32 devices in a mesh: row: 4 (over y, core), col: 8 (over z, x).
Axes of the slice: x: 2, y: 2, z: 4, core: 2. Of those that a mesh axis runs over, the one named last changes fastest.
Arguments:
- row_gen: bfloat16 [64, 1024, 256], P(('row', 'col')), may hold values from -6 to 6
- row_upd: bfloat16 [64, 1024, 256], P(('row', 'col')), may hold values from -6 to 6
- col_gen: bfloat16 [64, 1024, 256], P('row', 'col'), may hold values from -6 to 6
- col_upd: bfloat16 [64, 1024, 256], P('row', 'col'), may hold values from -6 to 6
- leaf_rank: int32 [64], P(('row', 'col')), may hold values from 32 to 256, as said below
- leaf_trunc: int32 [64], P(('row', 'col')), may hold values from 128 to 512
- node_trunc: int32 [4, 14], replicated, may hold values from 128 to 384, as said below
- coupling: float32 [2048, 512], P(('row', 'col')), may hold values from -6 to 6
Outputs:
- recompressed: float32 [2048, 512], P(('row', 'col'))
The draws below stay inside these ranges and needn't reach their ends.
Inputs may be any that keep to these rules, and one draw needn't show every extreme that they name: `leaf_rank`: the first leaf of every device (leaf indices that are multiples of 2) has rank 256. `node_trunc`: column 0 (the first height-0 node of each top node) is 384 in every row.
All inputs are finite; a program needn't handle non-finite values.
Results may differ from the reference program's by a relative error of at most 0.0003.
Values may be sent and summed in bfloat16 or wider, within the bound.
A program may use at most 128 MiB of HBM per device.

```python
import jax
import jax.numpy as jnp
from jax import lax

LEAF = 1024
RANK = 256
UPD = 256
LEAF_DEV = 2
KB = 512
TMAX = 384
LEAVES = 64
TOPS = 4
N_ROW = 4
N_COL = 8


def draw_leaf_rank(key, part):
    base_ranks = jax.random.randint(key, (LEAVES,), RANK // 8, RANK + 1)
    leading = jnp.arange(LEAVES) % LEAF_DEV == 0
    return jnp.where(leading, RANK, base_ranks).astype(jnp.int32)


def draw_node_trunc(key, part):
    base_ranks = jax.random.randint(key, (TOPS, 14), KB // 4, TMAX + 1)
    leading = jnp.arange(14)[None, :] == 0
    return jnp.where(leading, TMAX, base_ranks).astype(jnp.int32)


def with_ends(drawn, own_key, low, largest):
    longest = drawn.shape.index(max(drawn.shape))
    spots = []
    for shift in (0, 1):
        where = [jax.random.randint(jax.random.fold_in(own_key, axis), (), 0, length) for axis, length in enumerate(drawn.shape)]
        where[longest] = (where[longest] + shift) % drawn.shape[longest]
        spots.append(tuple(where))
    return drawn.at[spots[0]].set(low).at[spots[1]].set(largest)


def block_scale(rng, dims, pieces, smallest, high):
    loudness, own = 1.0, jax.random.fold_in(rng, 6)
    for axis_at, blocks in pieces:
        steps = jnp.exp(jax.random.uniform(jax.random.fold_in(own, axis_at), (blocks,), jnp.float32, smallest / len(pieces), high / len(pieces)))
        loudness = loudness * jnp.repeat(steps, dims[axis_at] // blocks).reshape([-1 if axis == axis_at else 1 for axis in range(len(dims))])
    return loudness


def normal_values(own_key, dims, scale, bound, shards=(), kind=jnp.bfloat16):
    values = jax.random.normal(own_key, dims, jnp.float32) * scale
    if len(shards) > 0:
        values = block_scale(own_key, dims, shards, -0.22, 0.18) * values
    return jnp.clip(values, min=-bound, max=bound).astype(kind)


def setup_inputs(seed: int = 0) -> dict:
    key_list = jax.random.split(jax.random.key(seed), 9)
    row_gen = normal_values(key_list[0], (LEAVES, LEAF, RANK), 1.0, 6.0, ((0, 32),))
    row_upd = normal_values(key_list[1], (LEAVES, LEAF, UPD), 1.0, 6.0, ((0, 32),))
    col_gen = normal_values(key_list[2], (LEAVES, LEAF, RANK), 1.0, 6.0, ((0, 4), (1, 8)))
    col_upd = normal_values(key_list[3], (LEAVES, LEAF, UPD), 1.0, 6.0, ((0, 4), (1, 8)))
    leaf_rank = draw_leaf_rank(jax.random.fold_in(key_list[8], 71), 0)
    leaf_trunc = with_ends(jax.random.randint(key_list[5], (LEAVES,), KB // 4, KB + 1), jax.random.fold_in(key_list[5], 1), KB // 4, KB).astype(jnp.int32)
    node_trunc = draw_node_trunc(jax.random.fold_in(key_list[8], 71), 0)
    coupling = normal_values(key_list[7], (TOPS * KB, KB), 1.0, 6.0, ((0, 32),), jnp.float32)
    return {"row_gen": row_gen, "row_upd": row_upd, "col_gen": col_gen, "col_upd": col_upd, "leaf_rank": leaf_rank, "leaf_trunc": leaf_trunc, "node_trunc": node_trunc, "coupling": coupling}


HIGH = lax.Precision.HIGHEST
OFFSETS = (0, 8, 12)

def device_factor(generator, update, ranks, truncs):
    width_gen = generator.shape[2]
    col_ids = jnp.arange(width_gen, dtype=jnp.int32)
    keep_cols = (col_ids[None, None, :] < ranks[:, None, None]).astype(jnp.float32)
    stacked = jnp.concatenate([generator.astype(jnp.float32) * keep_cols, update.astype(jnp.float32)], axis=2)
    gram_matrix = jnp.einsum('nlk,nlm->nkm', stacked, stacked, precision=HIGH)
    width_all = gram_matrix.shape[1]
    gram_matrix = gram_matrix + jnp.eye(width_all, dtype=jnp.float32)
    factor = jnp.swapaxes(jnp.linalg.cholesky(gram_matrix), 1, 2)
    row_ids = jnp.arange(width_all, dtype=jnp.int32)
    kept_rows = factor * (row_ids[None, :, None] < truncs[:, None, None]).astype(jnp.float32)
    node_gram = jnp.einsum('nrk,nrm->km', kept_rows, kept_rows, precision=HIGH) + jnp.eye(width_all, dtype=jnp.float32)
    return jnp.linalg.cholesky(node_gram).T

def merge_level(factors, limits):
    width_all = factors.shape[1]
    row_ids = jnp.arange(width_all, dtype=jnp.int32)
    kept_rows = factors * (row_ids[None, :, None] < limits[:, None, None]).astype(jnp.float32)
    first_child = kept_rows[0::2]
    second_child = kept_rows[1::2]
    gram_matrix = jnp.einsum('nrk,nrm->nkm', first_child, first_child, precision=HIGH)
    gram_matrix = gram_matrix + jnp.einsum('nrk,nrm->nkm', second_child, second_child, precision=HIGH)
    gram_matrix = gram_matrix + jnp.eye(width_all, dtype=jnp.float32)
    return jnp.swapaxes(jnp.linalg.cholesky(gram_matrix), 1, 2)

def reference(row_gen, row_upd, col_gen, col_upd, leaf_rank, leaf_trunc, node_trunc, coupling):

    def device_node(index):

        def piece(array):
            return lax.dynamic_slice_in_dim(array, (index * LEAF_DEV).astype(jnp.int32), LEAF_DEV, 0)
        ranks = piece(leaf_rank)
        truncs = piece(leaf_trunc)
        return (device_factor(piece(row_gen), piece(row_upd), ranks, truncs), device_factor(piece(col_gen), piece(col_upd), ranks, truncs))
    row_nodes, col_nodes = lax.map(device_node, jnp.arange(N_ROW * N_COL, dtype=jnp.int32))
    for height in range(3):
        node_ids = jnp.arange(row_nodes.shape[0], dtype=jnp.int32)
        span_nodes = 8 >> height
        limits = node_trunc[node_ids // span_nodes, OFFSETS[height] + node_ids % span_nodes]
        row_nodes = merge_level(row_nodes, limits)
        col_nodes = merge_level(col_nodes, limits)
    per_row = N_COL // 8
    top_ids = jnp.arange(TOPS, dtype=jnp.int32)
    partner_ids = jnp.bitwise_xor(top_ids // per_row, 1) * per_row + top_ids % per_row
    blocks = coupling.reshape(TOPS, KB, KB)
    product = jnp.einsum('gij,gjk->gik', row_nodes, blocks, precision=HIGH)
    product = jnp.einsum('gik,glk->gil', product, col_nodes[partner_ids], precision=HIGH)
    product = product / (8 * LEAF_DEV * LEAF)
    return product.reshape(TOPS * KB, KB)
```

```python
import functools

import jax
import jax.numpy as jnp
from jax import lax
from jax.experimental import pallas as pl
from jax.experimental.pallas import tpu as pltpu
from jax.sharding import PartitionSpec as P

HIGH = lax.Precision.HIGHEST
OFFSETS = (0, 8, 12)
B = 128
F32 = jnp.float32
BF16 = jnp.bfloat16


def split2(x):
    hi = x.astype(BF16)
    lo = (x - hi.astype(F32)).astype(BF16)
    return hi, lo


def split3(x):
    hi = x.astype(BF16)
    rest = x - hi.astype(F32)
    mid = rest.astype(BF16)
    lo = (rest - mid.astype(F32)).astype(BF16)
    return hi, mid, lo


def dot_tn(a, b):
    return lax.dot_general(a, b, (((0,), (0,)), ((), ())), preferred_element_type=F32)


def dot_nn(a, b):
    return jnp.dot(a, b, preferred_element_type=F32)


def gram3(x):
    hi, lo = split2(x)
    cross = dot_tn(hi, lo)
    return dot_tn(hi, hi) + cross + dot_tn(lo, hi)


def eliminate(v, w, p, sub):
    cols = [jnp.broadcast_to(v[:, 8 * p + j : 8 * p + j + 1], (8, B)) for j in range(8)]
    diag = cols[0]
    for j in range(8):
        pivot = jnp.broadcast_to(cols[j][j : j + 1, :], (8, B))
        if j:
            diag = jnp.where(sub == j, pivot, diag)
        else:
            diag = pivot
        if j == 7:
            break
        coef = jnp.where(sub > j, cols[j] / pivot, 0.0)
        for k in range(j + 1, 8):
            cols[k] = cols[k] - coef * jnp.broadcast_to(cols[k][j : j + 1, :], (8, B))
        v = v - coef * jnp.broadcast_to(v[j : j + 1, :], (8, B))
        w = w - coef * jnp.broadcast_to(w[j : j + 1, :], (8, B))
    scale = lax.rsqrt(diag)
    return v * scale, w * scale


def diag_factor(blocks):
    sub = lax.broadcasted_iota(jnp.int32, (8, B), 0)
    lane = lax.broadcasted_iota(jnp.int32, (8, B), 1)
    count = len(blocks)
    left = [[blk[8 * g : 8 * g + 8, :] for g in range(16)] for blk in blocks]
    right = [[jnp.where(lane == sub + 8 * g, 1.0, 0.0).astype(F32) for g in range(16)] for _ in blocks]
    for p in range(16):
        for n in range(count):
            v, w = eliminate(left[n][p], right[n][p], p, sub)
            v = jnp.where(lane >= sub + 8 * p, v, 0.0)
            left[n][p], right[n][p] = v, w
            if p == 15:
                continue
            turned = jnp.transpose(v, (1, 0))
            g = p + 1
            for r in range(8):
                coef = jnp.broadcast_to(turned[8 * g : 8 * g + 8, r : r + 1], (8, B))
                left[n][g] = left[n][g] - coef * jnp.broadcast_to(v[r : r + 1, :], (8, B))
                right[n][g] = right[n][g] - coef * jnp.broadcast_to(w[r : r + 1, :], (8, B))
            if p == 14:
                continue
            both = jnp.concatenate([v, w], axis=1)
            hi, mid, lo = split3(both)
            hv, mv, lv = hi[:, :B], mid[:, :B], lo[:, :B]
            lhs = jnp.concatenate([hv, mv, hv, mv, hv, lv], axis=0)
            rhs = jnp.concatenate([hi, hi, mid, mid, lo, hi], axis=0)
            change = dot_tn(lhs, rhs)
            for g in range(p + 2, 16):
                left[n][g] = left[n][g] - change[8 * g : 8 * g + 8, :B]
                right[n][g] = right[n][g] - change[8 * g : 8 * g + 8, B:]
    return [(jnp.concatenate(left[n], axis=0), jnp.concatenate(right[n], axis=0)) for n in range(count)]


def factor(refs, panels):
    width = refs[0].shape[1]

    def step(p, carry):
        start = pl.multiple_of(p * B, B)
        rows = pl.ds(start, B)
        done = diag_factor([ref[rows, rows] for ref in refs])
        col = lax.broadcasted_iota(jnp.int32, (B, width), 1)
        row = lax.broadcasted_iota(jnp.int32, (B, width), 0)
        his, los = [], []
        for ref, (_, inverse) in zip(refs, done):
            hi, lo = split2(ref[rows, :])
            ihi, ilo = split2(inverse)
            panel = dot_nn(ihi, hi) + dot_nn(ihi, lo) + dot_nn(ilo, hi)
            panel = jnp.where(col >= row + start, panel, 0.0)
            ref[rows, :] = panel
        for ref, (upper, _) in zip(refs, done):
            ref[rows, rows] = upper

        def trail(q, c):
            other = pl.ds(pl.multiple_of(q * B, B), B)
            for ref in refs:
                hi, lo = split2(ref[rows, :])
                qhi, qlo = split2(ref[rows, other])
                ref[other, :] = ref[other, :] - (dot_tn(qhi, hi) + dot_tn(qhi, lo) + dot_tn(qlo, hi))
            return c

        lax.fori_loop(p + 1, width // B, trail, 0)
        return carry

    lax.fori_loop(0, panels, step, 0)


def eye(width):
    return jnp.where(
        lax.broadcasted_iota(jnp.int32, (width, width), 0) == lax.broadcasted_iota(jnp.int32, (width, width), 1), 1.0, 0.0
    ).astype(F32)


def keep_rows(x, limit):
    return jnp.where(lax.broadcasted_iota(jnp.int32, x.shape, 0) < limit, x, 0.0)


def leaf_kernel(rank_ref, trunc_ref, node_ref, gen_ref, upd_ref, out_ref, *grams):
    leaves = gen_ref.shape[0]
    for i in range(leaves):
        gen = gen_ref[i]
        ids = lax.broadcasted_iota(jnp.int32, gen.shape, 1)
        gen = jnp.where(ids < rank_ref[i], gen.astype(F32), 0.0).astype(BF16)
        whole = jnp.concatenate([gen, upd_ref[i]], axis=1)
        grams[i][...] = dot_tn(whole, whole) + eye(whole.shape[1])
    width = grams[0].shape[0]
    factor(grams[:leaves], width // B)
    total = eye(width)
    for i in range(leaves):
        total = total + gram3(keep_rows(grams[i][...], trunc_ref[i]))
    grams[0][...] = total
    kept = out_ref.shape[0]
    factor(grams[:1], kept // B)
    out_ref[...] = keep_rows(grams[0][:kept, :], node_ref[0])


def merge_kernel(node_ref, own_ref, other_ref, out_ref, gram):
    width = gram.shape[0]
    gram[...] = eye(width) + gram3(own_ref[...]) + gram3(other_ref[...])
    kept = out_ref.shape[0]
    factor([gram], kept // B)
    out_ref[...] = keep_rows(gram[:kept, :], node_ref[0])


SMEM = pl.BlockSpec(memory_space=pltpu.SMEM)
VMEM = pl.BlockSpec(memory_space=pltpu.VMEM)
LIMIT = 56 * 1024 * 1024


def leaf_call(rank, trunc, node, gen, upd, kept):
    width = gen.shape[2] + upd.shape[2]
    return pl.pallas_call(
        leaf_kernel,
        out_shape=jax.ShapeDtypeStruct((kept, width), F32),
        in_specs=[SMEM, SMEM, SMEM, VMEM, VMEM],
        out_specs=VMEM,
        scratch_shapes=[pltpu.VMEM((width, width), F32)] * gen.shape[0],
        compiler_params=pltpu.CompilerParams(vmem_limit_bytes=LIMIT),
    )(rank, trunc, node, gen, upd)


def merge_call(node, own, other, kept):
    width = own.shape[1]
    return pl.pallas_call(
        merge_kernel,
        out_shape=jax.ShapeDtypeStruct((kept, width), F32),
        in_specs=[SMEM, VMEM, VMEM],
        out_specs=VMEM,
        scratch_shapes=[pltpu.VMEM((width, width), F32)],
        compiler_params=pltpu.CompilerParams(vmem_limit_bytes=LIMIT),
    )(node, own, other)


def swap(block, axis, distance):
    count = lax.axis_size(axis)
    return lax.ppermute(block, axis, [(i, i ^ distance) for i in range(count)])


def body(row_gen, row_upd, col_gen, col_upd, leaf_rank, leaf_trunc, node_trunc, coupling):
    width = row_gen.shape[2] + row_upd.shape[2]
    kept = 384
    columns = lax.axis_size("col")
    col_gen_full = lax.all_to_all(col_gen, "col", split_axis=0, concat_axis=1, tiled=True)
    col_upd_full = lax.all_to_all(col_upd, "col", split_axis=0, concat_axis=1, tiled=True)
    blocks = [[8 * i + j for j in range(8)] for i in range(columns // 8)]
    mine = lax.all_gather(coupling, "col", axis=0, tiled=True, axis_index_groups=blocks)
    row_pos = lax.axis_index("row")
    col_pos = lax.axis_index("col")
    top = row_pos * (columns // 8) + col_pos // 8
    member = col_pos % 8
    odd = member % 2 == 1
    limits = [node_trunc[top, OFFSETS[h] + (member >> h)][None] for h in range(3)]
    row_factor = leaf_call(leaf_rank, leaf_trunc, limits[0], row_gen, row_upd, kept)
    col_factor = leaf_call(leaf_rank, leaf_trunc, limits[0], col_gen_full, col_upd_full, kept)
    own = jnp.where(odd, col_factor, row_factor)
    other = swap(jnp.where(odd, row_factor, col_factor), "col", 1)
    own = merge_call(limits[1], own, other, kept)
    other = swap(own, "col", 2)
    own = merge_call(limits[2], own, other, kept)
    other = swap(own, "col", 4)
    full = jnp.full((1,), width, jnp.int32)
    top_factor = merge_call(full, own, other, width)
    partner = swap(top_factor, "row", 1)
    share = width // 4
    part = lax.dynamic_slice_in_dim(top_factor, member // 2 * share, share, 0)
    half = swap(jnp.dot(part, mine, precision=HIGH), "col", 1)
    result = lax.dot_general(half, partner, (((1,), (1,)), ((), ())), precision=HIGH)
    result = result / (8 * row_gen.shape[0] * row_gen.shape[1])
    back = swap(result[: share // 2], "col", 1)
    return jnp.where(odd, result[share // 2 :], back)


def solution(mesh):
    return jax.shard_map(
        body,
        mesh=mesh,
        in_specs=(
            P(("row", "col"), None, None),
            P(("row", "col"), None, None),
            P("row", "col", None),
            P("row", "col", None),
            P(("row", "col")),
            P(("row", "col")),
            P(),
            P(("row", "col"), None),
        ),
        out_specs=P(("row", "col"), None),
        check_vma=False,
    )
```

```python
import functools

import jax
import jax.numpy as jnp
from jax import lax
from jax.experimental import pallas as pl
from jax.experimental.pallas import tpu as pltpu
from jax.sharding import PartitionSpec as P

HIGH = lax.Precision.HIGHEST
OFFSETS = (0, 8, 12)
B = 128
F32 = jnp.float32
BF16 = jnp.bfloat16


def split2(x):
    hi = x.astype(BF16)
    lo = (x - hi.astype(F32)).astype(BF16)
    return hi, lo


def split3(x):
    hi = x.astype(BF16)
    rest = x - hi.astype(F32)
    mid = rest.astype(BF16)
    lo = (rest - mid.astype(F32)).astype(BF16)
    return hi, mid, lo


def dot_tn(a, b):
    return lax.dot_general(a, b, (((0,), (0,)), ((), ())), preferred_element_type=F32)


def dot_nn(a, b):
    return jnp.dot(a, b, preferred_element_type=F32)


def gram3(x):
    hi, lo = split2(x)
    cross = dot_tn(hi, lo)
    return dot_tn(hi, hi) + cross + dot_tn(lo, hi)


def recip(x):
    r = pltpu.reciprocal(x, approx=True)
    return r * (2.0 - x * r)


def sub_row(x, j):
    return jnp.broadcast_to(x[j : j + 1, :], (8, B))


def lane_col(x, k):
    return jnp.broadcast_to(x[:, k : k + 1], (8, B))


def diag_factor(blocks):
    sub = lax.broadcasted_iota(jnp.int32, (8, B), 0)
    lane = lax.broadcasted_iota(jnp.int32, (8, B), 1)
    every = range(len(blocks))
    G = 4 if len(blocks) == 1 else 2
    left = [[blk[8 * g : 8 * g + 8, :] for g in range(16)] for blk in blocks]
    right = [[jnp.where(lane == sub + 8 * g, 1.0, 0.0).astype(F32) for g in range(16)] for _ in blocks]
    count = 8 * G
    for p in range(0, 16, G):
        vs = [left[m][p : p + G] for m in every]
        ws = [right[m][p : p + G] for m in every]
        cols = [[[lane_col(vs[m][a], 8 * p + k) for k in range(8 * (a + 1))] for a in range(G)] for m in every]
        diag = [[None] * G for _ in every]
        for j in range(0, count, 2):
            ja, js = divmod(j, 8)
            for m in every:
                col, v, w = cols[m], vs[m], ws[m]
                d00 = sub_row(col[ja][j], js)
                d01 = sub_row(col[ja][j], js + 1)
                d11 = sub_row(col[ja][j + 1], js + 1)
                det = d00 * d11 - d01 * d01
                r0 = recip(d00)
                second = det * r0
                old = second if js == 0 else jnp.where(sub == js + 1, second, diag[m][ja])
                diag[m][ja] = jnp.where(sub == js, d00, old)
                inner = jnp.where(sub == js + 1, d01 * r0, 0.0)
                v0, v1 = sub_row(v[ja], js), sub_row(v[ja], js + 1)
                w0, w1 = sub_row(w[ja], js), sub_row(w[ja], js + 1)
                if js == 6:
                    v[ja] = v[ja] - inner * v0
                    w[ja] = w[ja] - inner * w0
                if j + 2 == count:
                    continue
                rdet = recip(det)
                for a in range(ja, G):
                    if a == ja and js == 6:
                        continue
                    x, y = col[a][j], col[a][j + 1]
                    px = (d11 * x - d01 * y) * rdet
                    py = (d00 * y - d01 * x) * rdet
                    if a == ja:
                        px = jnp.where(sub > js + 1, px, 0.0)
                        py = jnp.where(sub > js + 1, py, 0.0)
                    for k in range(j + 2, 8 * (a + 1)):
                        ka, ks = divmod(k, 8)
                        col[a][k] = col[a][k] - (px * sub_row(col[ka][j], ks) + py * sub_row(col[ka][j + 1], ks))
                    if a == ja:
                        px = px + inner
                    v[a] = v[a] - (px * v0 + py * v1)
                    w[a] = w[a] - (px * w0 + py * w1)
        for m in every:
            v, w = vs[m], ws[m]
            for a in range(G):
                scale = lax.rsqrt(diag[m][a])
                v[a] = jnp.where(lane >= sub + 8 * (p + a), v[a] * scale, 0.0)
                w[a] = w[a] * scale
                left[m][p + a], right[m][p + a] = v[a], w[a]
            if p + G == 16:
                continue
            both = jnp.concatenate([jnp.concatenate(v, axis=0), jnp.concatenate(w, axis=0)], axis=1)
            hi, mid, lo = split3(both)
            hv, mv, lv = hi[:, :B], mid[:, :B], lo[:, :B]
            lhs = jnp.concatenate([hv, mv, hv, mv, hv, lv], axis=0)
            rhs = jnp.concatenate([hi, hi, mid, mid, lo, hi], axis=0)
            change = dot_tn(lhs, rhs)
            for g in range(p + G, 16):
                left[m][g] = left[m][g] - change[8 * g : 8 * g + 8, :B]
                right[m][g] = right[m][g] - change[8 * g : 8 * g + 8, B:]
    return [(jnp.concatenate(left[m], axis=0), jnp.concatenate(right[m], axis=0)) for m in every]


def factor(refs, panels):
    width = refs[0].shape[1]

    def step(p, carry):
        start = pl.multiple_of(p * B, B)
        rows = pl.ds(start, B)
        done = diag_factor([ref[rows, rows] for ref in refs])
        col = lax.broadcasted_iota(jnp.int32, (B, width), 1)
        row = lax.broadcasted_iota(jnp.int32, (B, width), 0)
        his, los = [], []
        for ref, (_, inverse) in zip(refs, done):
            hi, lo = split2(ref[rows, :])
            ihi, ilo = split2(inverse)
            panel = dot_nn(ihi, hi) + dot_nn(ihi, lo) + dot_nn(ilo, hi)
            panel = jnp.where(col >= row + start, panel, 0.0)
            ref[rows, :] = panel
        for ref, (upper, _) in zip(refs, done):
            ref[rows, rows] = upper

        def trail(q, c):
            other = pl.ds(pl.multiple_of(q * B, B), B)
            for ref in refs:
                hi, lo = split2(ref[rows, :])
                qhi, qlo = split2(ref[rows, other])
                ref[other, :] = ref[other, :] - (dot_tn(qhi, hi) + dot_tn(qhi, lo) + dot_tn(qlo, hi))
            return c

        lax.fori_loop(p + 1, width // B, trail, 0)
        return carry

    lax.fori_loop(0, panels, step, 0)


def eye(width):
    return jnp.where(
        lax.broadcasted_iota(jnp.int32, (width, width), 0) == lax.broadcasted_iota(jnp.int32, (width, width), 1), 1.0, 0.0
    ).astype(F32)


def keep_rows(x, limit):
    return jnp.where(lax.broadcasted_iota(jnp.int32, x.shape, 0) < limit, x, 0.0)


def leaf_kernel(rank_ref, trunc_ref, node_ref, gen_ref, upd_ref, out_ref, *grams):
    leaves = gen_ref.shape[0]
    for i in range(leaves):
        gen = gen_ref[i]
        ids = lax.broadcasted_iota(jnp.int32, gen.shape, 1)
        gen = jnp.where(ids < rank_ref[i], gen.astype(F32), 0.0).astype(BF16)
        whole = jnp.concatenate([gen, upd_ref[i]], axis=1)
        grams[i][...] = dot_tn(whole, whole) + eye(whole.shape[1])
    width = grams[0].shape[0]
    factor(grams[:leaves], width // B)
    total = eye(width)
    for i in range(leaves):
        total = total + gram3(keep_rows(grams[i][...], trunc_ref[i]))
    grams[0][...] = total
    kept = out_ref.shape[0]
    factor(grams[:1], kept // B)
    out_ref[...] = keep_rows(grams[0][:kept, :], node_ref[0])


def merge_kernel(node_ref, own_ref, other_ref, out_ref, gram):
    width = gram.shape[0]
    gram[...] = eye(width) + gram3(own_ref[...]) + gram3(other_ref[...])
    kept = out_ref.shape[0]
    factor([gram], kept // B)
    out_ref[...] = keep_rows(gram[:kept, :], node_ref[0])


SMEM = pl.BlockSpec(memory_space=pltpu.SMEM)
VMEM = pl.BlockSpec(memory_space=pltpu.VMEM)
LIMIT = 56 * 1024 * 1024


def leaf_call(rank, trunc, node, gen, upd, kept):
    width = gen.shape[2] + upd.shape[2]
    return pl.pallas_call(
        leaf_kernel,
        out_shape=jax.ShapeDtypeStruct((kept, width), F32),
        in_specs=[SMEM, SMEM, SMEM, VMEM, VMEM],
        out_specs=VMEM,
        scratch_shapes=[pltpu.VMEM((width, width), F32)] * gen.shape[0],
        compiler_params=pltpu.CompilerParams(vmem_limit_bytes=LIMIT),
        cost_estimate=pl.CostEstimate(flops=50_000_000_000, bytes_accessed=100_000_000, transcendentals=0),
    )(rank, trunc, node, gen, upd)


def merge_call(node, own, other, kept):
    width = own.shape[1]
    return pl.pallas_call(
        merge_kernel,
        out_shape=jax.ShapeDtypeStruct((kept, width), F32),
        in_specs=[SMEM, VMEM, VMEM],
        out_specs=VMEM,
        scratch_shapes=[pltpu.VMEM((width, width), F32)],
        compiler_params=pltpu.CompilerParams(vmem_limit_bytes=LIMIT),
    )(node, own, other)


def swap(block, axis, distance):
    count = lax.axis_size(axis)
    return lax.ppermute(block, axis, [(i, i ^ distance) for i in range(count)])


def body(row_gen, row_upd, col_gen, col_upd, leaf_rank, leaf_trunc, node_trunc, coupling):
    width = row_gen.shape[2] + row_upd.shape[2]
    kept = 384
    columns = lax.axis_size("col")
    col_both = jnp.concatenate([col_gen, col_upd], axis=2)
    col_full = lax.all_to_all(col_both, "col", split_axis=0, concat_axis=1, tiled=True)
    cut = col_gen.shape[2]
    blocks = [[8 * i + j for j in range(8)] for i in range(columns // 8)]
    mine = lax.all_gather(coupling, "col", axis=0, tiled=True, axis_index_groups=blocks)
    row_pos = lax.axis_index("row")
    col_pos = lax.axis_index("col")
    top = row_pos * (columns // 8) + col_pos // 8
    member = col_pos % 8
    odd = member % 2 == 1
    limits = [node_trunc[top, OFFSETS[h] + (member >> h)][None] for h in range(3)]
    row_factor = leaf_call(leaf_rank, leaf_trunc, limits[0], row_gen, row_upd, kept)
    col_factor = leaf_call(leaf_rank, leaf_trunc, limits[0], col_full[:, :, :cut], col_full[:, :, cut:], kept)
    own = jnp.where(odd, col_factor, row_factor)
    other = swap(jnp.where(odd, row_factor, col_factor), "col", 1)
    own = merge_call(limits[1], own, other, kept)
    other = swap(own, "col", 2)
    own = merge_call(limits[2], own, other, kept)
    other = swap(own, "col", 4)
    full = jnp.full((1,), width, jnp.int32)
    top_factor = merge_call(full, own, other, width)
    partner = swap(top_factor, "row", 1)
    share = width // 4
    part = lax.dynamic_slice_in_dim(top_factor, member // 2 * share, share, 0)
    half = swap(jnp.dot(part, mine, precision=HIGH), "col", 1)
    result = lax.dot_general(half, partner, (((1,), (1,)), ((), ())), precision=HIGH)
    result = result / (8 * row_gen.shape[0] * row_gen.shape[1])
    back = swap(result[: share // 2], "col", 1)
    return jnp.where(odd, result[share // 2 :], back)


def solution(mesh):
    return jax.shard_map(
        body,
        mesh=mesh,
        in_specs=(
            P(("row", "col"), None, None),
            P(("row", "col"), None, None),
            P("row", "col", None),
            P("row", "col", None),
            P(("row", "col")),
            P(("row", "col")),
            P(),
            P(("row", "col"), None),
        ),
        out_specs=P(("row", "col"), None),
        check_vma=False,
    )
```

```python
import functools

import jax
import jax.numpy as jnp
from jax import lax
from jax.experimental import pallas as pl
from jax.experimental.pallas import tpu as pltpu
from jax.sharding import PartitionSpec as P

HIGH = lax.Precision.HIGHEST
OFFSETS = (0, 8, 12)
B = 128
F32 = jnp.float32
BF16 = jnp.bfloat16


def split2(x):
    hi = x.astype(BF16)
    lo = (x - hi.astype(F32)).astype(BF16)
    return hi, lo


def split3(x):
    hi = x.astype(BF16)
    rest = x - hi.astype(F32)
    mid = rest.astype(BF16)
    lo = (rest - mid.astype(F32)).astype(BF16)
    return hi, mid, lo


def dot_tn(a, b):
    return lax.dot_general(a, b, (((0,), (0,)), ((), ())), preferred_element_type=F32)


def dot_nn(a, b):
    return jnp.dot(a, b, preferred_element_type=F32)


def gram3(x):
    hi, lo = split2(x)
    cross = dot_tn(hi, lo)
    return dot_tn(hi, hi) + cross + dot_tn(lo, hi)


def recip(x):
    r = pltpu.reciprocal(x, approx=True)
    return r * (2.0 - x * r)


def sub_row(x, j):
    return jnp.broadcast_to(x[j : j + 1, :], (8, B))


def lane_col(x, k):
    return jnp.broadcast_to(x[:, k : k + 1], (8, B))


def diag_factor(blocks):
    sub = lax.broadcasted_iota(jnp.int32, (8, B), 0)
    lane = lax.broadcasted_iota(jnp.int32, (8, B), 1)
    every = range(len(blocks))
    G = 4 if len(blocks) == 1 else 2
    left = [[blk[8 * g : 8 * g + 8, :] for g in range(16)] for blk in blocks]
    right = [[jnp.where(lane == sub + 8 * g, 1.0, 0.0).astype(F32) for g in range(16)] for _ in blocks]
    count = 8 * G
    for p in range(0, 16, G):
        vs = [left[m][p : p + G] for m in every]
        ws = [right[m][p : p + G] for m in every]
        cols = [[[lane_col(vs[m][a], 8 * p + k) for k in range(8 * (a + 1))] for a in range(G)] for m in every]
        diag = [[None] * G for _ in every]
        for j in range(0, count, 2):
            ja, js = divmod(j, 8)
            for m in every:
                col, v, w = cols[m], vs[m], ws[m]
                d00 = sub_row(col[ja][j], js)
                d01 = sub_row(col[ja][j], js + 1)
                d11 = sub_row(col[ja][j + 1], js + 1)
                det = d00 * d11 - d01 * d01
                r0 = recip(d00)
                second = det * r0
                old = second if js == 0 else jnp.where(sub == js + 1, second, diag[m][ja])
                diag[m][ja] = jnp.where(sub == js, d00, old)
                inner = jnp.where(sub == js + 1, d01 * r0, 0.0)
                v0, v1 = sub_row(v[ja], js), sub_row(v[ja], js + 1)
                w0, w1 = sub_row(w[ja], js), sub_row(w[ja], js + 1)
                if js == 6:
                    v[ja] = v[ja] - inner * v0
                    w[ja] = w[ja] - inner * w0
                if j + 2 == count:
                    continue
                rdet = recip(det)
                for a in range(ja, G):
                    if a == ja and js == 6:
                        continue
                    x, y = col[a][j], col[a][j + 1]
                    px = (d11 * x - d01 * y) * rdet
                    py = (d00 * y - d01 * x) * rdet
                    if a == ja:
                        px = jnp.where(sub > js + 1, px, 0.0)
                        py = jnp.where(sub > js + 1, py, 0.0)
                    for k in range(j + 2, 8 * (a + 1)):
                        ka, ks = divmod(k, 8)
                        col[a][k] = col[a][k] - (px * sub_row(col[ka][j], ks) + py * sub_row(col[ka][j + 1], ks))
                    if a == ja:
                        px = px + inner
                    v[a] = v[a] - (px * v0 + py * v1)
                    w[a] = w[a] - (px * w0 + py * w1)
        for m in every:
            v, w = vs[m], ws[m]
            for a in range(G):
                scale = lax.rsqrt(diag[m][a])
                v[a] = jnp.where(lane >= sub + 8 * (p + a), v[a] * scale, 0.0)
                w[a] = w[a] * scale
                left[m][p + a], right[m][p + a] = v[a], w[a]
            if p + G == 16:
                continue
            both = jnp.concatenate([jnp.concatenate(v, axis=0), jnp.concatenate(w, axis=0)], axis=1)
            hi, mid, lo = split3(both)
            hv, mv, lv = hi[:, :B], mid[:, :B], lo[:, :B]
            lhs = jnp.concatenate([hv, mv, hv, mv, hv, lv], axis=0)
            rhs = jnp.concatenate([hi, hi, mid, mid, lo, hi], axis=0)
            change = dot_tn(lhs, rhs)
            for g in range(p + G, 16):
                left[m][g] = left[m][g] - change[8 * g : 8 * g + 8, :B]
                right[m][g] = right[m][g] - change[8 * g : 8 * g + 8, B:]
    return [(jnp.concatenate(left[m], axis=0), jnp.concatenate(right[m], axis=0)) for m in every]


def factor(refs, panels, after=None):
    width = refs[0].shape[1]

    def step(p, carry):
        start = pl.multiple_of(p * B, B)
        rows = pl.ds(start, B)
        done = diag_factor([ref[rows, rows] for ref in refs])
        col = lax.broadcasted_iota(jnp.int32, (B, width), 1)
        row = lax.broadcasted_iota(jnp.int32, (B, width), 0)
        his, los = [], []
        for ref, (_, inverse) in zip(refs, done):
            hi, lo = split2(ref[rows, :])
            ihi, ilo = split2(inverse)
            panel = dot_nn(ihi, hi) + dot_nn(ihi, lo) + dot_nn(ilo, hi)
            panel = jnp.where(col >= row + start, panel, 0.0)
            ref[rows, :] = panel
        for ref, (upper, _) in zip(refs, done):
            ref[rows, rows] = upper

        def trail(q, c):
            other = pl.ds(pl.multiple_of(q * B, B), B)
            for ref in refs:
                hi, lo = split2(ref[rows, :])
                qhi, qlo = split2(ref[rows, other])
                ref[other, :] = ref[other, :] - (dot_tn(qhi, hi) + dot_tn(qhi, lo) + dot_tn(qlo, hi))
            return c

        if after is not None:
            after(p)
        lax.fori_loop(p + 1, width // B, trail, 0)
        return carry

    lax.fori_loop(0, panels, step, 0)


def eye(width):
    return jnp.where(
        lax.broadcasted_iota(jnp.int32, (width, width), 0) == lax.broadcasted_iota(jnp.int32, (width, width), 1), 1.0, 0.0
    ).astype(F32)


def keep_rows(x, limit):
    return jnp.where(lax.broadcasted_iota(jnp.int32, x.shape, 0) < limit, x, 0.0)


KEPT = 3


def leaf_total(rank_ref, trunc_ref, gen_ref, upd_ref, grams):
    leaves = gen_ref.shape[0]
    for i in range(leaves):
        gen = gen_ref[i]
        ids = lax.broadcasted_iota(jnp.int32, gen.shape, 1)
        gen = jnp.where(ids < rank_ref[i], gen.astype(F32), 0.0).astype(BF16)
        whole = jnp.concatenate([gen, upd_ref[i]], axis=1)
        grams[i][...] = dot_tn(whole, whole) + eye(whole.shape[1])
    width = grams[0].shape[0]
    factor(grams, width // B)
    total = eye(width)
    for i in range(leaves):
        total = total + gram3(keep_rows(grams[i][...], trunc_ref[i]))
    grams[0][...] = total


def kept_panel(gram, p, limit):
    return keep_rows(gram[p * B : (p + 1) * B, p * B :], limit - p * B)


def leaf_kernel(rank_ref, trunc_ref, node_ref, gen_ref, upd_ref, *refs):
    outs, grams = refs[:KEPT], refs[KEPT:]
    leaf_total(rank_ref, trunc_ref, gen_ref, upd_ref, grams)
    factor(grams[:1], KEPT)
    for p in range(KEPT):
        outs[p][...] = kept_panel(grams[0], p, node_ref[0])


def tree_kernel(rank_ref, trunc_ref, node_ref, gen_ref, upd_ref, *refs):
    rows, out_ref, refs = refs[:KEPT], refs[KEPT], refs[KEPT + 1 :]
    grams, refs = refs[: gen_ref.shape[0]], refs[gen_ref.shape[0] :]
    own, send, land = refs[:KEPT], refs[KEPT : 2 * KEPT], refs[2 * KEPT : 3 * KEPT]
    send_sem, recv_sem = refs[3 * KEPT :]
    gram = grams[0]
    width = gram.shape[0]
    place = lax.axis_index("col")
    odd = place % 2
    partners = [place + d * (1 - 2 * ((place // d) % 2)) for d in (1, 2, 4)]

    barrier = pltpu.get_barrier_semaphore()
    for other in partners:
        pl.semaphore_signal(barrier, inc=1, device_id={"col": other}, device_id_type=pl.DeviceIdType.MESH)
    pl.semaphore_wait(barrier, 3)

    def copy(h, p):
        return pltpu.make_async_remote_copy(
            src_ref=send[p].at[h],
            dst_ref=land[p].at[h],
            send_sem=send_sem.at[h, p],
            recv_sem=recv_sem.at[h, p],
            device_id={"col": partners[h]},
            device_id_type=pl.DeviceIdType.MESH,
        )

    leaf_total(rank_ref, trunc_ref, gen_ref, upd_ref, grams)

    def level(h, carry):
        def after(p):
            for c in range(KEPT):

                @pl.when((p == c) & (h == 0))
                def _(c=c):
                    mine = kept_panel(gram, c, node_ref[0])

                    @pl.when(odd == 1)
                    def _():
                        own[c][...] = mine
                        send[c][0] = rows[c][...]

                    @pl.when(odd == 0)
                    def _():
                        own[c][...] = rows[c][...]
                        send[c][0] = mine

                    copy(0, c).start()

                for hh in (1, 2):

                    @pl.when((p == c) & (h == hh))
                    def _(c=c, hh=hh):
                        mine = kept_panel(gram, c, node_ref[hh])
                        own[c][...] = mine
                        send[c][hh] = mine
                        copy(hh, c).start()

        factor([gram], KEPT + h // 3, after)

        @pl.when(h < 3)
        def _():
            gram[...] = eye(width)
            for p in range(KEPT):
                gram[p * B :, p * B :] = gram[p * B :, p * B :] + gram3(own[p][...])

        for p in range(KEPT):
            for hh in range(3):

                @pl.when(h == hh)
                def _(p=p, hh=hh):
                    copy(hh, p).wait()
                    gram[p * B :, p * B :] = gram[p * B :, p * B :] + gram3(land[p][hh])

        return carry

    lax.fori_loop(0, 4, level, 0)
    out_ref[...] = gram[...]


SMEM = pl.BlockSpec(memory_space=pltpu.SMEM)
VMEM = pl.BlockSpec(memory_space=pltpu.VMEM)
LIMIT = 56 * 1024 * 1024


def panel_shapes(width, lead=()):
    return [lead + (B, width - p * B) for p in range(KEPT)]


def leaf_call(rank, trunc, node, gen, upd):
    width = gen.shape[2] + upd.shape[2]
    return pl.pallas_call(
        leaf_kernel,
        out_shape=[jax.ShapeDtypeStruct(shape, F32) for shape in panel_shapes(width)],
        in_specs=[SMEM, SMEM, SMEM, VMEM, VMEM],
        out_specs=[VMEM] * KEPT,
        scratch_shapes=[pltpu.VMEM((width, width), F32)] * gen.shape[0],
        compiler_params=pltpu.CompilerParams(vmem_limit_bytes=LIMIT),
        cost_estimate=pl.CostEstimate(flops=50_000_000_000, bytes_accessed=100_000_000, transcendentals=0),
    )(rank, trunc, node, gen, upd)


def tree_call(rank, trunc, node, gen, upd, rows):
    width = gen.shape[2] + upd.shape[2]
    return pl.pallas_call(
        tree_kernel,
        out_shape=jax.ShapeDtypeStruct((width, width), F32),
        in_specs=[SMEM, SMEM, SMEM, VMEM, VMEM] + [VMEM] * KEPT,
        out_specs=VMEM,
        scratch_shapes=[pltpu.VMEM((width, width), F32)] * gen.shape[0]
        + [pltpu.VMEM(shape, F32) for shape in panel_shapes(width)]
        + [pltpu.VMEM(shape, F32) for shape in panel_shapes(width, (3,))] * 2
        + [pltpu.SemaphoreType.DMA((3, KEPT)), pltpu.SemaphoreType.DMA((3, KEPT))],
        compiler_params=pltpu.CompilerParams(vmem_limit_bytes=LIMIT, collective_id=0, has_side_effects=True),
        cost_estimate=pl.CostEstimate(flops=50_000_000_000, bytes_accessed=100_000_000, transcendentals=0),
    )(rank, trunc, node, gen, upd, *rows)


def swap(block, axis, distance):
    count = lax.axis_size(axis)
    return lax.ppermute(block, axis, [(i, i ^ distance) for i in range(count)])


def body(row_gen, row_upd, col_gen, col_upd, leaf_rank, leaf_trunc, node_trunc, coupling):
    width = row_gen.shape[2] + row_upd.shape[2]
    columns = lax.axis_size("col")
    col_both = jnp.concatenate([col_gen, col_upd], axis=2)
    col_full = lax.all_to_all(col_both, "col", split_axis=0, concat_axis=1, tiled=True)
    cut = col_gen.shape[2]
    blocks = [[8 * i + j for j in range(8)] for i in range(columns // 8)]
    mine = lax.all_gather(coupling, "col", axis=0, tiled=True, axis_index_groups=blocks)
    row_pos = lax.axis_index("row")
    col_pos = lax.axis_index("col")
    top = row_pos * (columns // 8) + col_pos // 8
    member = col_pos % 8
    odd = member % 2 == 1
    limits = jnp.stack([node_trunc[top, OFFSETS[h] + (member >> h)] for h in range(3)])
    rows = leaf_call(leaf_rank, leaf_trunc, limits, row_gen, row_upd)
    top_factor = tree_call(leaf_rank, leaf_trunc, limits, col_full[:, :, :cut], col_full[:, :, cut:], rows)
    partner = swap(top_factor, "row", 1)
    share = width // 4
    part = lax.dynamic_slice_in_dim(top_factor, member // 2 * share, share, 0)
    half = swap(jnp.dot(part, mine, precision=HIGH), "col", 1)
    result = lax.dot_general(half, partner, (((1,), (1,)), ((), ())), precision=HIGH)
    result = result / (8 * row_gen.shape[0] * row_gen.shape[1])
    back = swap(result[: share // 2], "col", 1)
    return jnp.where(odd, result[share // 2 :], back)


def solution(mesh):
    return jax.shard_map(
        body,
        mesh=mesh,
        in_specs=(
            P(("row", "col"), None, None),
            P(("row", "col"), None, None),
            P("row", "col", None),
            P("row", "col", None),
            P(("row", "col")),
            P(("row", "col")),
            P(),
            P(("row", "col"), None),
        ),
        out_specs=P(("row", "col"), None),
        check_vma=False,
    )
```
